32 devices in a mesh: dp: 4 (over y, x), expert: 8 (over z, core).
Axes of the slice: x: 2, y: 2, z: 4, core: 2. Of those that a mesh axis runs over, the one named last changes fastest.
Arguments:
- tokens: bfloat16 [1024, 4096], P('dp', 'expert'), may hold values from -6 to 6
- out_grads: bfloat16 [1024, 4096], P('dp', 'expert'), may hold values from -6 to 6
- routes: int32 [1024, 2], P('dp'), may hold values from 0 to 7, all different within a row; in each aligned block of 256 rows (0 to 255, 256 to 511, ...) at most 64 rows name the same one
- gate_codes: int32 [1024, 2], P('dp'), may hold values from 256 to 4095
- w_gate: bfloat16 [8, 4096, 6400], P('expert', None, 'dp'), may hold values from -0.09375 to 0.09375
- w_up: bfloat16 [8, 4096, 6400], P('expert', None, 'dp'), may hold values from -0.09375 to 0.09375
- w_down: bfloat16 [8, 6400, 4096], P('expert', 'dp'), may hold values from -0.078125 to 0.078125
- proj_in: bfloat16 [4096, 128], replicated, may hold values from -0.09375 to 0.09375
- proj_hidden: bfloat16 [6400, 192], P('dp'), may hold values from -0.078125 to 0.078125
Outputs:
- projected: float32 [4, 8, 12288], P(None, 'expert', 'dp')
The draws below stay inside these ranges and needn't reach their ends.
Inputs may be any that keep to these rules, and one draw needn't show every extreme that they name: `routes`: each row names 2 different experts. Among the rows of one sequence no expert is named more than 64 times, a bound that some block reaches.
All inputs are finite; a program needn't handle non-finite values.
Results may differ from the reference program's by a relative error of at most 0.0029.
Values may be sent and summed in bfloat16 or wider, within the bound.
A program may use at most 128 MiB of HBM per device.

```python
import math
import jax
import jax.numpy as jnp
import numpy as np
from jax import lax

D = 4096
FF = 6400
TOP = 2
R = 64
LEN = 256
SEQS = 4
CAP = 64
EXPERTS = 8
TOKENS = 1024


def set_ends(array, key, low, high):
    longest = array.shape.index(max(array.shape))
    spots = []
    for shift in (0, 1):
        where = [jax.random.randint(jax.random.fold_in(key, axis), (), 0, length) for axis, length in enumerate(array.shape)]
        where[longest] = (where[longest] + shift) % array.shape[longest]
        spots.append(tuple(where))
    return array.at[spots[0]].set(low).at[spots[1]].set(high)


def level_of(key, dims, cuts, low, top_value):
    def one(axis_at, blocks):
        steps = jax.random.uniform(jax.random.fold_in(jax.random.fold_in(key, 6), axis_at), (blocks,), jnp.float32, low / len(cuts), top_value / len(cuts))
        return jnp.repeat(jnp.exp(steps), dims[axis_at] // blocks).reshape((-1,) + (1,) * (len(dims) - axis_at - 1))

    factor_of = one(*cuts[0])
    for cut in cuts[1:]:
        factor_of = factor_of * one(*cut)
    return factor_of


def deal_out(own_key, own, number, rows, number_of, top, bound, lean):
    sequence = jax.random.permutation(own_key, number_of)
    crowded, ordinary = load_shares(number_of, rows * top, bound, lean, True), load_shares(number_of, rows * top, bound, lean, False)
    places = jnp.arange(number_of)

    def named(lengths, offset_by):
        used = int((lengths > 0).sum())
        fixed = max(1, used // 4)
        moved = fixed + (places - fixed + offset_by * (used - fixed)) % max(1, number_of - fixed)
        return jnp.zeros((number_of,), jnp.int32).at[sequence[jnp.where(places < fixed, places, moved)]].set(jnp.asarray(lengths, jnp.int32))

    lengths = jnp.where(number % 4 == 0, named(crowded, number // 4), named(ordinary, number - number // 4 - 1))
    mixed = jax.random.permutation(jax.random.fold_in(own, 3), number_of)
    source_of, taker = mixed[0:number_of // 2 * 2:2], mixed[1:number_of // 2 * 2:2]
    room = jnp.minimum(lengths[source_of] - 1, bound - lengths[taker]) // 2
    room = jnp.where((source_of == sequence[0]) | (taker == sequence[0]) | (lengths[taker] == 0), 0, jnp.maximum(room, 0))
    moved = jax.random.randint(jax.random.fold_in(own, 4), (number_of // 2,), 0, 1 << 20) % (room + 1)
    lengths = lengths.at[source_of].add(-moved).at[taker].add(moved)
    items = jnp.searchsorted(jnp.cumsum(lengths), jnp.arange(rows * top), side="right").astype(jnp.int32)
    table = items.reshape(top, rows).T
    table = table[jax.random.permutation(jax.random.fold_in(own, 1), rows)]
    offset_by = jax.random.randint(jax.random.fold_in(own, 2), (rows, 1), 0, top)
    return jnp.take_along_axis(table, (jnp.arange(top)[None, :] + offset_by) % top, axis=1)


def load_shares(count, total, bound, slope, full):
    weights = [(1 << 20) // math.isqrt(grade ** slope) + 1 for grade in range(1, count + 1)]
    largest = bound if full else min(bound, max(-(-total // count), total * weights[0] // sum(weights)))
    least = 1 if total - largest >= count - 1 else 0
    counts, spare = [largest] + [least] * (count - 1), total - largest - least * (count - 1)
    while spare > 0:
        candidates = [i for i in range(1, count) if counts[i] < largest] or [i for i in range(1, count) if counts[i] < bound]
        whole, remaining = sum([weights[i] for i in candidates]), spare
        for i in candidates:
            more = min(bound - counts[i], max(1, remaining * weights[i] // whole), spare)
            counts[i] = counts[i] + more
            spare = spare - more
    return np.array(counts)


def normal_values(stream_key, extent, scale, reach, cuts=(), kind=jnp.bfloat16):
    gain = level_of(stream_key, extent, cuts, -0.22, 0.18) if cuts else 1.0
    result = jax.random.normal(stream_key, extent, jnp.float32) * scale * gain
    return jnp.minimum(jnp.maximum(result, -reach), reach).astype(kind)


def setup_inputs(seed: int = 0) -> dict:
    arg_keys = jax.random.split(jax.random.key(seed), 10)
    tokens = normal_values(arg_keys[0], (TOKENS, D), 1.0, 6.0, ((0, 4), (1, 8)))
    out_grads = normal_values(arg_keys[1], (TOKENS, D), 1.0, 6.0, ((0, 4), (1, 8)))
    routes_keys = jax.random.split(jax.random.fold_in(arg_keys[2], 1), TOKENS // LEN)
    routes_turns = jax.random.permutation(jax.random.fold_in(arg_keys[2], 3), TOKENS // LEN)
    routes = jax.vmap(lambda own, number: deal_out(jax.random.fold_in(arg_keys[2], 2), own, number, LEN, EXPERTS, TOP, CAP, 2))(routes_keys, routes_turns).reshape((TOKENS, TOP))
    gate_codes = set_ends(jax.random.randint(arg_keys[3], (TOKENS, TOP), 256, 4096), jax.random.fold_in(arg_keys[3], 1), 256, 4095).astype(jnp.int32)
    w_gate = normal_values(arg_keys[4], (EXPERTS, D, FF), D ** -0.5, 0.09375, ((0, 8), (2, 4)))
    w_up = normal_values(arg_keys[5], (EXPERTS, D, FF), D ** -0.5, 0.09375, ((0, 8), (2, 4)))
    w_down = normal_values(arg_keys[6], (EXPERTS, FF, D), FF ** -0.5, 0.078125, ((0, 8), (1, 4)))
    proj_in = normal_values(arg_keys[7], (D, 2 * R), D ** -0.5, 0.09375)
    proj_hidden = normal_values(arg_keys[8], (FF, 3 * R), FF ** -0.5, 0.078125, ((0, 4),))
    return {"tokens": tokens, "out_grads": out_grads, "routes": routes, "gate_codes": gate_codes, "w_gate": w_gate, "w_up": w_up, "w_down": w_down, "proj_in": proj_in, "proj_hidden": proj_hidden}


def expert_grads(xs, dys, weight, seq_ids, wg, wu, wd, proj_in, proj_hidden):
    rank = proj_in.shape[1] // 2
    gate = jnp.dot(xs, wg, preferred_element_type=jnp.float32)
    upper = jnp.dot(xs, wu, preferred_element_type=jnp.float32)
    sig = jax.nn.sigmoid(gate)
    act = gate * sig
    hidden = (act * upper).astype(jnp.bfloat16)
    back = lax.dot_general(dys, wd, (((1,), (1,)), ((), ())), preferred_element_type=jnp.float32) * weight[:, None]
    d_up = (back * act).astype(jnp.bfloat16)
    d_gate = (back * upper * sig * (1.0 + gate * (1.0 - sig))).astype(jnp.bfloat16)
    in_proj = jnp.dot(xs, proj_in[:, :rank], preferred_element_type=jnp.float32)
    out_proj = jnp.dot(dys, proj_in[:, rank:], preferred_element_type=jnp.float32) * weight[:, None]
    hid_proj = jnp.dot(hidden, proj_hidden[:, :rank], preferred_element_type=jnp.float32)
    gate_proj = jnp.dot(d_gate, proj_hidden[:, rank:2 * rank], preferred_element_type=jnp.float32)
    up_proj = jnp.dot(d_up, proj_hidden[:, 2 * rank:], preferred_element_type=jnp.float32)
    onehot = (seq_ids[:, None] == jnp.arange(SEQS, dtype=jnp.int32)[None, :]).astype(jnp.float32)
    lefts = jnp.stack([in_proj, in_proj, hid_proj])
    rights = jnp.stack([gate_proj, up_proj, out_proj])
    total = jnp.einsum('ns,knr,knq->skrq', onehot, lefts, rights, precision=lax.Precision.HIGHEST)
    return total.reshape(SEQS, 3 * rank * rank)


def reference(tokens, out_grads, routes, gate_codes, w_gate, w_up, w_down, proj_in, proj_hidden):
    most = SEQS * CAP

    def one_expert(index):
        code = jnp.sum(jnp.where(routes == index, gate_codes, 0), axis=1).astype(jnp.int32)
        order = jnp.argsort(jnp.where(code > 0, 0, 1).astype(jnp.int32), stable=True)[:most].astype(jnp.int32)
        picked = code[order]
        weight = picked.astype(jnp.float32) / 4096.0
        seq_ids = jnp.where(picked > 0, order // LEN, -1).astype(jnp.int32)
        return expert_grads(tokens[order], out_grads[order], weight, seq_ids,
                            w_gate[index], w_up[index], w_down[index], proj_in, proj_hidden)

    stacked = lax.map(one_expert, jnp.arange(EXPERTS, dtype=jnp.int32))
    return jnp.transpose(stacked, (1, 0, 2))
```

```python
import functools
import math

import jax
import jax.numpy as jnp
from jax import lax
from jax.experimental import pallas as pl
from jax.experimental.pallas import tpu as pltpu
from jax.sharding import PartitionSpec as P

MESH = pl.DeviceIdType.MESH
TILE = 256
LAG = 3


def swapped(a, b, count):
    total, bit = 0, 1
    while bit < count:
        total = total + lax.rem(lax.div(a, bit) + lax.div(b, bit), 2) * bit
        bit *= 2
    return total


def kernel(
    n_dp, n_exp, tokens, grads, routes, codes, w_gate, w_up, w_down, proj_in, proj_hidden, out,
    packed, slots, gate_w, up_w, down_w, gate, upper, back, in_sum, out_sum, hid_sum, weight_rows, parts, arrived,
    load_sem, send_one, recv_one, send_two, recv_two, recv_three, send_row, recv_row, send_part, recv_part,
):
    rows, chunk = tokens.shape
    cap = packed.shape[1]
    hidden = gate.shape[1]
    rank = proj_in.shape[1] // 2
    side = math.isqrt(n_dp)
    units = 2 * n_exp
    total_rows = n_dp * cap
    seq = lax.axis_index("dp")
    mine = lax.axis_index("expert")
    seq_y, seq_x = lax.div(seq, side), lax.rem(seq, side)

    def at_seq(index):
        return lax.rem(seq + index, n_dp)

    barrier = pltpu.get_barrier_semaphore()
    for step in range(1, n_dp):
        pl.semaphore_signal(barrier, inc=1, device_id=(at_seq(step), mine), device_id_type=MESH)
    for step in range(1, n_exp):
        pl.semaphore_signal(
            barrier, inc=1, device_id=(seq, lax.rem(mine + step, n_exp)), device_id_type=MESH
        )

    def weight_copy(which, j):
        span = pl.ds(pl.multiple_of(j * chunk, chunk), chunk)
        if which == 0:
            return pltpu.make_async_copy(w_gate.at[0, span, :], gate_w.at[j], load_sem.at[0, j])
        if which == 1:
            return pltpu.make_async_copy(w_up.at[0, span, :], up_w.at[j], load_sem.at[1, j])
        return pltpu.make_async_copy(w_down.at[0, :, span], down_w.at[j], load_sem.at[2, j])

    def load_x(k, carry):
        j = swapped(mine, k, n_exp)
        weight_copy(0, j).start()
        weight_copy(1, j).start()
        return carry

    def load_dy(k, carry):
        weight_copy(2, swapped(mine, k, n_exp)).start()
        return carry

    lax.fori_loop(0, n_exp, load_x, 0)
    lax.fori_loop(0, n_exp, load_dy, 0)

    lanes = max(128, n_exp)
    experts = lax.broadcasted_iota(jnp.int32, (rows, lanes), 1)
    first, second = routes[:, 0:1], routes[:, 1:2]
    hit = jnp.where((first == experts) | (second == experts), 1.0, 0.0)
    earlier = jnp.where(
        lax.broadcasted_iota(jnp.int32, (rows, rows), 1) < lax.broadcasted_iota(jnp.int32, (rows, rows), 0), 1.0, 0.0
    )
    place = jnp.dot(
        earlier.astype(jnp.bfloat16), hit.astype(jnp.bfloat16), preferred_element_type=jnp.float32
    )
    key = jnp.where(hit > 0.5, place, -1.0)
    keys = key.T
    slot_ids = lax.broadcasted_iota(jnp.int32, (cap, rows), 0).astype(jnp.float32)
    picks = jnp.concatenate(
        [jnp.where(keys[e : e + 1, :] == slot_ids, 1.0, 0.0).astype(jnp.bfloat16) for e in range(n_exp)], axis=0
    )
    for a, source in enumerate((tokens, grads)):
        values = jnp.dot(picks, source[...], preferred_element_type=jnp.float32).astype(jnp.bfloat16)
        packed[a * n_exp : (a + 1) * n_exp] = values.reshape(n_exp, cap, chunk)
        slots[a * n_exp + mine, seq] = packed[a * n_exp + mine]

    own_key = jnp.sum(jnp.where(experts == mine, key, 0.0), axis=1, keepdims=True)
    own_code = jnp.where(first == mine, codes[:, 0:1], 0) + jnp.where(second == mine, codes[:, 1:2], 0)
    slot_lanes = lax.broadcasted_iota(jnp.int32, (rows, 128), 1).astype(jnp.float32)
    own_weight = own_code.astype(jnp.float32) / 4096.0
    row = jnp.sum(jnp.where(own_key == slot_lanes, own_weight, 0.0), axis=0, keepdims=True)
    weight_rows[seq] = jnp.broadcast_to(row, (8, 128))

    pl.semaphore_wait(barrier, n_dp - 1 + n_exp - 1)

    def send_block(src, dst, send_sem, recv_sem, to_seq, to_expert):
        pltpu.make_async_remote_copy(
            src_ref=src, dst_ref=dst, send_sem=send_sem, recv_sem=recv_sem,
            device_id=(to_seq, to_expert), device_id_type=MESH,
        ).start()

    def wait_for(ref, sem):
        pltpu.make_async_copy(ref, ref, sem).wait()

    def peers(k):
        odd = lax.rem(k, 2)
        one, two = [], []
        for step in range(1, side):
            along_x = seq_y * side + lax.rem(seq_x + step, side)
            along_y = lax.rem(seq_y + step, side) * side + seq_x
            one.append(along_x + odd * (along_y - along_x))
            two.append(along_y + odd * (along_x - along_y))
        return one, two

    def split(unit):
        a, k = lax.div(unit, n_exp), lax.rem(unit, n_exp)
        return a, k, a * n_exp + swapped(mine, k, n_exp)

    def send_out(a):
        def body(k, carry):
            to = swapped(mine, k, n_exp)
            send_block(
                packed.at[a * n_exp + to], slots.at[a * n_exp + mine, seq],
                send_one, recv_one.at[a * n_exp + mine], seq, to,
            )
            return carry
        return body

    def stage_one(unit):
        a, k, at = split(unit)

        @pl.when(k > 0)
        def _():
            wait_for(slots.at[at, seq], recv_one.at[at])

        one, two = peers(k)
        for to in one:
            send_block(slots.at[at, seq], slots.at[at, seq], send_two, recv_two.at[at], to, mine)
        for to in two:
            send_block(slots.at[at, seq], slots.at[at, seq], send_two, recv_three.at[at], to, mine)

    def stage_two(unit):
        a, k, at = split(unit)
        one, two = peers(k)
        wait_for(slots.at[at, pl.ds(0, side - 1)], recv_two.at[at])
        for source in one:
            for to in two:
                send_block(slots.at[at, source], slots.at[at, source], send_two, recv_three.at[at], to, mine)

    def tiles():
        return [(n, min(TILE, hidden - n)) for n in range(0, hidden, TILE)]

    def stage_three(unit):
        a, k, at = split(unit)
        j = swapped(mine, k, n_exp)
        wait_for(slots.at[at, pl.ds(0, side * (side - 1))], recv_three.at[at])
        span = pl.ds(pl.multiple_of(j * chunk, chunk), chunk)

        @pl.when(a == 0)
        def _():
            weight_copy(0, j).wait()
            weight_copy(1, j).wait()
            block = slots[at].reshape(total_rows, chunk)
            in_sum[...] += jnp.dot(block, proj_in[span, :], preferred_element_type=jnp.float32)
            for n, width in tiles():
                cols = slice(n, n + width)
                gate[:, cols] += jnp.dot(block, gate_w[j, :, cols], preferred_element_type=jnp.float32)
                upper[:, cols] += jnp.dot(block, up_w[j, :, cols], preferred_element_type=jnp.float32)

        @pl.when(a == 1)
        def _():
            weight_copy(2, j).wait()
            block = slots[at].reshape(total_rows, chunk)
            out_sum[...] += jnp.dot(block, proj_in[span, :], preferred_element_type=jnp.float32)
            for n, width in tiles():
                cols = slice(n, n + width)
                back[:, cols] += lax.dot_general(
                    block, down_w[j, cols, :], (((1,), (1,)), ((), ())), preferred_element_type=jnp.float32
                )

        @pl.when(unit == n_exp - 1)
        def _():
            for n, width in tiles():
                cols = slice(n, n + width)
                g, u = gate[:, cols], upper[:, cols]
                sig = jax.nn.sigmoid(g)
                act = g * sig
                hid_sum[...] += jnp.dot(
                    (act * u).astype(jnp.bfloat16), proj_hidden[cols, :rank], preferred_element_type=jnp.float32
                )
                gate[:, cols] = act
                upper[:, cols] = u * sig * (1.0 + g * (1.0 - sig))

    lax.fori_loop(1, n_exp, send_out(0), 0)
    for step in range(1, n_dp):
        send_block(weight_rows.at[seq], weight_rows.at[seq], send_row, recv_row, at_seq(step), mine)
    lax.fori_loop(1, n_exp, send_out(1), 0)
    for ref in (gate, upper, back, in_sum, out_sum, hid_sum):
        ref[...] = jnp.zeros_like(ref)

    def body(step, carry):
        pl.when(step < units)(lambda: stage_one(step))
        pl.when((step >= 1) & (step <= units))(lambda: stage_two(step - 1))
        pl.when(step >= LAG)(lambda: stage_three(step - LAG))
        return carry

    lax.fori_loop(0, units + LAG, body, 0)

    wait_for(weight_rows.at[pl.ds(0, n_dp - 1)], recv_row)
    diagonal = lax.broadcasted_iota(jnp.int32, (cap, 128), 0) == lax.broadcasted_iota(jnp.int32, (cap, 128), 1)
    weight = jnp.concatenate(
        [
            jnp.sum(jnp.where(diagonal, weight_rows[s, 0:1, :], 0.0), axis=1, keepdims=True)
            for s in range(n_dp)
        ],
        axis=0,
    )
    gate_proj = jnp.zeros((total_rows, rank), jnp.float32)
    up_proj = jnp.zeros((total_rows, rank), jnp.float32)
    for n, width in tiles():
        cols = slice(n, n + width)
        scaled = back[:, cols] * weight
        up_proj += jnp.dot(
            (scaled * gate[:, cols]).astype(jnp.bfloat16), proj_hidden[cols, 2 * rank :],
            preferred_element_type=jnp.float32,
        )
        gate_proj += jnp.dot(
            (scaled * upper[:, cols]).astype(jnp.bfloat16), proj_hidden[cols, rank : 2 * rank],
            preferred_element_type=jnp.float32,
        )
    in_proj = in_sum[:, :rank]
    out_proj = out_sum[:, rank:] * weight
    hid_proj = hid_sum[...]
    share = 3 * rank // n_dp

    def product(left, right):
        return lax.dot_general(
            left, right, (((0,), (0,)), ((), ())),
            preferred_element_type=jnp.float32, precision=lax.Precision.HIGHEST,
        )

    for s in range(n_dp):
        part = slice(s * cap, (s + 1) * cap)
        stacked = jnp.concatenate(
            [
                product(in_proj[part], gate_proj[part]),
                product(in_proj[part], up_proj[part]),
                product(hid_proj[part], out_proj[part]),
            ],
            axis=0,
        )
        for d in range(n_dp):
            parts[d, s] = stacked[d * share : (d + 1) * share]
    for step in range(1, n_dp):
        to = at_seq(step)
        send_block(parts.at[to], arrived.at[seq], send_part, recv_part, to, mine)
    arrived[seq] = parts[seq]
    wait_for(arrived.at[pl.ds(0, n_dp - 1)], recv_part)
    result = arrived[0]
    for s in range(1, n_dp):
        result += arrived[s]
    out[...] = result

    wait_for(packed.at[pl.ds(0, 2 * (n_exp - 1))], send_one)
    wait_for(slots.at[:, pl.ds(0, n_dp - 1)], send_two)
    wait_for(weight_rows.at[pl.ds(0, n_dp - 1)], send_row)
    wait_for(parts.at[pl.ds(0, n_dp - 1)], send_part)


def per_device(tokens, out_grads, routes, gate_codes, w_gate, w_up, w_down, proj_in, proj_hidden):
    n_dp = lax.axis_size("dp")
    n_exp = lax.axis_size("expert")
    rows, chunk = tokens.shape
    cap = rows // 4
    hidden = w_gate.shape[2]
    rank = proj_in.shape[1] // 2
    share = 3 * rank // n_dp
    total = n_dp * cap
    vmem = pl.BlockSpec(memory_space=pltpu.VMEM)
    hbm = pl.BlockSpec(memory_space=pl.ANY)
    f32, bf16 = jnp.float32, jnp.bfloat16
    dma = pltpu.SemaphoreType.DMA
    result = pl.pallas_call(
        functools.partial(kernel, n_dp, n_exp),
        out_shape=jax.ShapeDtypeStruct((n_dp, share, rank), f32),
        in_specs=[vmem, vmem, vmem, vmem, hbm, hbm, hbm, vmem, vmem],
        out_specs=vmem,
        scratch_shapes=[
            pltpu.VMEM((2 * n_exp, cap, chunk), bf16),
            pltpu.VMEM((2 * n_exp, n_dp, cap, chunk), bf16),
            pltpu.VMEM((n_exp, chunk, hidden), bf16),
            pltpu.VMEM((n_exp, chunk, hidden), bf16),
            pltpu.VMEM((n_exp, hidden, chunk), bf16),
            pltpu.VMEM((total, hidden), f32),
            pltpu.VMEM((total, hidden), f32),
            pltpu.VMEM((total, hidden), f32),
            pltpu.VMEM((total, 2 * rank), f32),
            pltpu.VMEM((total, 2 * rank), f32),
            pltpu.VMEM((total, rank), f32),
            pltpu.VMEM((n_dp, 8, 128), f32),
            pltpu.VMEM((n_dp, n_dp, share, rank), f32),
            pltpu.VMEM((n_dp, n_dp, share, rank), f32),
            dma((3, n_exp)),
            dma, dma((2 * n_exp,)),
            dma, dma((2 * n_exp,)), dma((2 * n_exp,)),
            dma, dma,
            dma, dma,
        ],
        compiler_params=pltpu.CompilerParams(
            collective_id=0, has_side_effects=True, vmem_limit_bytes=60 * 1024 * 1024
        ),
    )(tokens, out_grads, routes, gate_codes, w_gate, w_up, w_down, proj_in, proj_hidden)
    return result.reshape(n_dp, 1, share * rank)


def solution(mesh):
    return jax.shard_map(
        per_device,
        mesh=mesh,
        in_specs=(
            P("dp", "expert"),
            P("dp", "expert"),
            P("dp", None),
            P("dp", None),
            P("expert", None, "dp"),
            P("expert", None, "dp"),
            P("expert", "dp", None),
            P(),
            P("dp", None),
        ),
        out_specs=P(None, "expert", "dp"),
        check_vma=False,
    )
```

```python
import functools
import math

import jax
import jax.numpy as jnp
from jax import lax
from jax.experimental import pallas as pl
from jax.experimental.pallas import tpu as pltpu
from jax.sharding import PartitionSpec as P

MESH = pl.DeviceIdType.MESH
TILE = 400
LAG = 3


def swapped(a, b, count):
    total, bit = 0, 1
    while bit < count:
        total = total + lax.rem(lax.div(a, bit) + lax.div(b, bit), 2) * bit
        bit *= 2
    return total


def kernel(
    n_dp, n_exp, tokens, grads, routes, codes, w_gate, w_up, w_down, proj_in, proj_hidden, out,
    packed, slots, gate_w, up_w, down_w, gate, upper, back, in_sum, out_sum, hid_sum, squeezed, other, weight_rows, parts, arrived,
    load_sem, send_one, recv_one, send_two, recv_two, recv_three, send_row, recv_row, send_part, recv_part,
):
    rows, chunk = tokens.shape
    cap = packed.shape[1]
    hidden = gate.shape[0]
    rank = proj_in.shape[1] // 2
    side = math.isqrt(n_dp)
    units = 2 * n_exp
    total_rows = n_dp * cap
    seq = lax.axis_index("dp")
    mine = lax.axis_index("expert")
    seq_y, seq_x = lax.div(seq, side), lax.rem(seq, side)

    def at_seq(index):
        return lax.rem(seq + index, n_dp)

    barrier = pltpu.get_barrier_semaphore()
    for step in range(1, n_dp):
        pl.semaphore_signal(barrier, inc=1, device_id=(at_seq(step), mine), device_id_type=MESH)
    for step in range(1, n_exp):
        pl.semaphore_signal(
            barrier, inc=1, device_id=(seq, lax.rem(mine + step, n_exp)), device_id_type=MESH
        )

    def weight_copy(which, j):
        span = pl.ds(pl.multiple_of(j * chunk, chunk), chunk)
        source, target = ((w_gate, gate_w), (w_up, up_w), (w_down, down_w))[which]
        return pltpu.make_async_copy(source.at[0, :, span], target.at[j], load_sem.at[which, j])

    def load_x(k, carry):
        j = swapped(mine, k, n_exp)
        weight_copy(0, j).start()
        weight_copy(1, j).start()
        return carry

    def load_dy(k, carry):
        weight_copy(2, swapped(mine, k, n_exp)).start()
        return carry

    lax.fori_loop(0, n_exp, load_x, 0)
    lax.fori_loop(0, n_exp, load_dy, 0)

    depth = max(16, n_exp)
    experts = lax.broadcasted_iota(jnp.int32, (depth, rows), 0)
    first, second = routes[0:1, :], routes[1:2, :]
    hit = jnp.where((first == experts) | (second == experts), 1.0, 0.0)
    earlier = jnp.where(
        lax.broadcasted_iota(jnp.int32, (rows, rows), 0) < lax.broadcasted_iota(jnp.int32, (rows, rows), 1), 1.0, 0.0
    )
    place = jnp.dot(
        hit.astype(jnp.bfloat16), earlier.astype(jnp.bfloat16), preferred_element_type=jnp.float32
    )
    keys = jnp.where(hit > 0.5, place, -1.0)
    slot_ids = lax.broadcasted_iota(jnp.int32, (cap, rows), 0).astype(jnp.float32)
    picks = jnp.concatenate(
        [jnp.where(keys[e : e + 1, :] == slot_ids, 1.0, 0.0).astype(jnp.bfloat16) for e in range(n_exp)], axis=0
    )
    for a, source in enumerate((tokens, grads)):
        values = jnp.dot(picks, source[...], preferred_element_type=jnp.float32).astype(jnp.bfloat16)
        packed[a * n_exp : (a + 1) * n_exp] = values.reshape(n_exp, cap, chunk)
        slots[a * n_exp + mine, seq] = packed[a * n_exp + mine]

    own_key = jnp.sum(jnp.where(experts == mine, keys, 0.0), axis=0, keepdims=True)
    own_code = jnp.where(first == mine, codes[0:1, :], 0) + jnp.where(second == mine, codes[1:2, :], 0)
    own_weight = own_code.astype(jnp.float32) / 4096.0
    column = jnp.sum(jnp.where(own_key == slot_ids, own_weight, 0.0), axis=1, keepdims=True)
    diagonal = lax.broadcasted_iota(jnp.int32, (cap, 128), 0) == lax.broadcasted_iota(jnp.int32, (cap, 128), 1)
    row = jnp.sum(jnp.where(diagonal, column, 0.0), axis=0, keepdims=True)
    weight_rows[seq] = jnp.broadcast_to(row, (8, 128))

    pl.semaphore_wait(barrier, n_dp - 1 + n_exp - 1)

    def send_block(src, dst, send_sem, recv_sem, to_seq, to_expert):
        pltpu.make_async_remote_copy(
            src_ref=src, dst_ref=dst, send_sem=send_sem, recv_sem=recv_sem,
            device_id=(to_seq, to_expert), device_id_type=MESH,
        ).start()

    def wait_for(ref, sem):
        pltpu.make_async_copy(ref, ref, sem).wait()

    def peers(k):
        odd = lax.rem(k, 2)
        one, two = [], []
        for step in range(1, side):
            along_x = seq_y * side + lax.rem(seq_x + step, side)
            along_y = lax.rem(seq_y + step, side) * side + seq_x
            one.append(along_x + odd * (along_y - along_x))
            two.append(along_y + odd * (along_x - along_y))
        return one, two

    def split(unit):
        a, k = lax.div(unit, n_exp), lax.rem(unit, n_exp)
        return a, k, a * n_exp + swapped(mine, k, n_exp)

    def send_out(a):
        def body(k, carry):
            to = swapped(mine, k, n_exp)
            send_block(
                packed.at[a * n_exp + to], slots.at[a * n_exp + mine, seq],
                send_one, recv_one.at[a * n_exp + mine], seq, to,
            )
            return carry
        return body

    def stage_one(unit):
        a, k, at = split(unit)

        @pl.when(k > 0)
        def _():
            wait_for(slots.at[at, seq], recv_one.at[at])

        one, two = peers(k)
        for to in one:
            send_block(slots.at[at, seq], slots.at[at, seq], send_two, recv_two.at[at], to, mine)
        for to in two:
            send_block(slots.at[at, seq], slots.at[at, seq], send_two, recv_three.at[at], to, mine)

    def stage_two(unit):
        a, k, at = split(unit)
        one, two = peers(k)
        wait_for(slots.at[at, pl.ds(0, side - 1)], recv_two.at[at])
        for source in one:
            for to in two:
                send_block(slots.at[at, source], slots.at[at, source], send_two, recv_three.at[at], to, mine)

    tiles = [slice(n, min(n + TILE, hidden)) for n in range(0, hidden, TILE)]

    def stage_three(unit):
        a, k, at = split(unit)
        j = swapped(mine, k, n_exp)
        wait_for(slots.at[at, pl.ds(0, side * (side - 1))], recv_three.at[at])
        span = pl.ds(pl.multiple_of(j * chunk, chunk), chunk)

        @pl.when(a == 0)
        def _():
            weight_copy(0, j).wait()
            weight_copy(1, j).wait()
            block = slots[at].reshape(total_rows, chunk)
            in_sum[...] += jnp.dot(block, proj_in[span, :], preferred_element_type=jnp.float32)
            turned = block.T
            for part in tiles:
                gate[part] += jnp.dot(gate_w[j, part, :], turned, preferred_element_type=jnp.float32)
                upper[part] += jnp.dot(up_w[j, part, :], turned, preferred_element_type=jnp.float32)

        @pl.when(a == 1)
        def _():
            weight_copy(2, j).wait()
            block = slots[at].reshape(total_rows, chunk)
            out_sum[...] += jnp.dot(block, proj_in[span, :], preferred_element_type=jnp.float32)
            turned = block.T
            for part in tiles:
                back[part] += jnp.dot(down_w[j, part, :], turned, preferred_element_type=jnp.float32)

        @pl.when(unit == n_exp - 1)
        def _():
            for part in tiles:
                g, u = gate[part], upper[part]
                sig = jax.nn.sigmoid(g)
                act = g * sig
                gate[part] = act
                upper[part] = u * sig * (1.0 + g * (1.0 - sig))
                squeezed[part] = (act * u).astype(jnp.bfloat16)
            hid_sum[...] = jnp.dot(proj_hidden[:rank], squeezed[...], preferred_element_type=jnp.float32)

    lax.fori_loop(1, n_exp, send_out(0), 0)
    for step in range(1, n_dp):
        send_block(weight_rows.at[seq], weight_rows.at[seq], send_row, recv_row, at_seq(step), mine)
    lax.fori_loop(1, n_exp, send_out(1), 0)
    for ref in (gate, upper, back, in_sum, out_sum):
        ref[...] = jnp.zeros_like(ref)

    def body(step, carry):
        pl.when(step < units)(lambda: stage_one(step))
        pl.when((step >= 1) & (step <= units))(lambda: stage_two(step - 1))
        pl.when(step >= LAG)(lambda: stage_three(step - LAG))
        return carry

    lax.fori_loop(0, units + LAG, body, 0)

    wait_for(weight_rows.at[pl.ds(0, n_dp - 1)], recv_row)
    weight = jnp.concatenate([weight_rows[s, 0:1, :cap] for s in range(n_dp)], axis=1)
    for part in tiles:
        scaled = back[part] * weight
        squeezed[part] = (scaled * gate[part]).astype(jnp.bfloat16)
        other[part] = (scaled * upper[part]).astype(jnp.bfloat16)
    up_proj = jnp.dot(proj_hidden[2 * rank :], squeezed[...], preferred_element_type=jnp.float32)
    gate_proj = jnp.dot(proj_hidden[rank : 2 * rank], other[...], preferred_element_type=jnp.float32)
    in_proj = in_sum[...].T[:rank]
    out_proj = out_sum[...].T[rank:] * weight
    share = 3 * rank // n_dp

    shape = (n_dp * rank, total_rows)
    same = lax.div(lax.broadcasted_iota(jnp.int32, shape, 0), rank) == lax.div(
        lax.broadcasted_iota(jnp.int32, shape, 1), cap
    )

    def product(left, right):
        return lax.dot_general(
            left, right, (((1,), (1,)), ((), ())),
            preferred_element_type=jnp.float32, precision=lax.Precision.HIGHEST,
        )

    left_in = jnp.where(same, jnp.concatenate([in_proj] * n_dp, axis=0), 0.0)
    left_hid = jnp.where(same, jnp.concatenate([hid_sum[...]] * n_dp, axis=0), 0.0)
    products = (product(left_in, gate_proj), product(left_in, up_proj), product(left_hid, out_proj))
    for s in range(n_dp):
        stacked = jnp.concatenate([value[s * rank : (s + 1) * rank] for value in products], axis=0)
        for d in range(n_dp):
            parts[d, s] = stacked[d * share : (d + 1) * share]
    for step in range(1, n_dp):
        to = at_seq(step)
        send_block(parts.at[to], arrived.at[seq], send_part, recv_part, to, mine)
    arrived[seq] = parts[seq]
    wait_for(arrived.at[pl.ds(0, n_dp - 1)], recv_part)
    result = arrived[0]
    for s in range(1, n_dp):
        result += arrived[s]
    out[...] = result

    wait_for(packed.at[pl.ds(0, 2 * (n_exp - 1))], send_one)
    wait_for(slots.at[:, pl.ds(0, n_dp - 1)], send_two)
    wait_for(weight_rows.at[pl.ds(0, n_dp - 1)], send_row)
    wait_for(parts.at[pl.ds(0, n_dp - 1)], send_part)


def per_device(tokens, out_grads, routes, gate_codes, w_gate, w_up, w_down, proj_in, proj_hidden):
    n_dp = lax.axis_size("dp")
    n_exp = lax.axis_size("expert")
    rows, chunk = tokens.shape
    cap = rows // 4
    hidden = w_gate.shape[2]
    rank = proj_in.shape[1] // 2
    share = 3 * rank // n_dp
    total = n_dp * cap
    vmem = pl.BlockSpec(memory_space=pltpu.VMEM)
    hbm = pl.BlockSpec(memory_space=pl.ANY)
    f32, bf16 = jnp.float32, jnp.bfloat16
    dma = pltpu.SemaphoreType.DMA
    result = pl.pallas_call(
        functools.partial(kernel, n_dp, n_exp),
        out_shape=jax.ShapeDtypeStruct((n_dp, share, rank), f32),
        in_specs=[vmem, vmem, vmem, vmem, hbm, hbm, hbm, vmem, vmem],
        out_specs=vmem,
        scratch_shapes=[
            pltpu.VMEM((2 * n_exp, cap, chunk), bf16),
            pltpu.VMEM((2 * n_exp, n_dp, cap, chunk), bf16),
            pltpu.VMEM((n_exp, hidden, chunk), bf16),
            pltpu.VMEM((n_exp, hidden, chunk), bf16),
            pltpu.VMEM((n_exp, hidden, chunk), bf16),
            pltpu.VMEM((hidden, total), f32),
            pltpu.VMEM((hidden, total), f32),
            pltpu.VMEM((hidden, total), f32),
            pltpu.VMEM((total, 2 * rank), f32),
            pltpu.VMEM((total, 2 * rank), f32),
            pltpu.VMEM((rank, total), f32),
            pltpu.VMEM((hidden, total), bf16),
            pltpu.VMEM((hidden, total), bf16),
            pltpu.VMEM((n_dp, 8, 128), f32),
            pltpu.VMEM((n_dp, n_dp, share, rank), f32),
            pltpu.VMEM((n_dp, n_dp, share, rank), f32),
            dma((3, n_exp)),
            dma, dma((2 * n_exp,)),
            dma, dma((2 * n_exp,)), dma((2 * n_exp,)),
            dma, dma,
            dma, dma,
        ],
        compiler_params=pltpu.CompilerParams(
            collective_id=0, has_side_effects=True, vmem_limit_bytes=60 * 1024 * 1024
        ),
    )(
        tokens, out_grads, routes.T, gate_codes.T, jnp.swapaxes(w_gate, 1, 2), jnp.swapaxes(w_up, 1, 2), w_down,
        proj_in, proj_hidden.T,
    )
    return result.reshape(n_dp, 1, share * rank)


def solution(mesh):
    return jax.shard_map(
        per_device,
        mesh=mesh,
        in_specs=(
            P("dp", "expert"),
            P("dp", "expert"),
            P("dp", None),
            P("dp", None),
            P("expert", None, "dp"),
            P("expert", None, "dp"),
            P("expert", "dp", None),
            P(),
            P("dp", None),
        ),
        out_specs=P(None, "expert", "dp"),
        check_vma=False,
    )
```

```python
import functools
import math

import jax
import jax.numpy as jnp
from jax import lax
from jax.experimental import pallas as pl
from jax.experimental.pallas import tpu as pltpu
from jax.sharding import PartitionSpec as P

MESH = pl.DeviceIdType.MESH
TILE = 400
AHEAD = 8
LOADS = 4
RELAY = 2
LAG = 4


def swapped(a, b, count):
    total, bit = 0, 1
    while bit < count:
        total = total + lax.rem(lax.div(a, bit) + lax.div(b, bit), 2) * bit
        bit *= 2
    return total


def kernel(
    n_dp, n_exp, tokens, grads, routes, codes, w_gate, w_up, w_down, proj_in_hbm, proj_hidden_hbm, out,
    packed, slots, gate_w, up_w, down_w, gate, upper, back, in_sum, out_sum, hid_sum, squeezed, other, proj_in, proj_hidden, weight_rows, parts, arrived,
    load_sem, proj_sem, send_one, recv_one, send_two, recv_two, recv_three, send_row, recv_row, send_part, recv_part,
):
    rows, chunk = tokens.shape
    cap = packed.shape[1]
    hidden = gate.shape[0]
    rank = proj_in_hbm.shape[1] // 2
    side = math.isqrt(n_dp)
    units = 2 * n_exp
    total_rows = n_dp * cap
    seq = lax.axis_index("dp")
    mine = lax.axis_index("expert")
    seq_y, seq_x = lax.div(seq, side), lax.rem(seq, side)

    def at_seq(index):
        return lax.rem(seq + index, n_dp)

    barrier = pltpu.get_barrier_semaphore()
    for step in range(1, n_dp):
        pl.semaphore_signal(barrier, inc=1, device_id=(at_seq(step), mine), device_id_type=MESH)
    for step in range(1, n_exp):
        pl.semaphore_signal(
            barrier, inc=1, device_id=(seq, lax.rem(mine + step, n_exp)), device_id_type=MESH
        )

    def weight_copy(which, j):
        span = pl.ds(pl.multiple_of(j * chunk, chunk), chunk)
        source, target = ((w_gate, gate_w), (w_up, up_w), (w_down, down_w))[which]
        return pltpu.make_async_copy(source.at[0, :, span], target.at[j], load_sem.at[which, j])

    projections = (
        pltpu.make_async_copy(proj_in_hbm, proj_in, proj_sem.at[0]),
        pltpu.make_async_copy(proj_hidden_hbm, proj_hidden, proj_sem.at[1]),
    )

    def split(unit):
        base, size, edge = 0, 2, 4
        while edge < units:
            past = lax.div(lax.div(unit, edge) + units, units + 1)
            base = base + past * (edge if edge == 4 else edge // 2)
            size = size + past * (0 if edge == 4 else edge // 4)
            edge *= 2
        within = unit - base
        a = lax.div(within, size)
        k = lax.rem(within, size) + size * lax.div(lax.div(unit, 4) + units, units + 1)
        return a, k, a * n_exp + swapped(mine, k, n_exp)

    def load(unit):
        a, k, _ = split(unit)
        j = swapped(mine, k, n_exp)

        @pl.when(a == 0)
        def _():
            weight_copy(0, j).start()
            weight_copy(1, j).start()

        @pl.when(a == 1)
        def _():
            weight_copy(2, j).start()

    depth = max(16, n_exp)
    experts = lax.broadcasted_iota(jnp.int32, (depth, rows), 0)
    first, second = routes[0:1, :], routes[1:2, :]
    hit = jnp.where((first == experts) | (second == experts), 1.0, 0.0)
    earlier = jnp.where(
        lax.broadcasted_iota(jnp.int32, (rows, rows), 0) < lax.broadcasted_iota(jnp.int32, (rows, rows), 1), 1.0, 0.0
    )
    place = jnp.dot(
        hit.astype(jnp.bfloat16), earlier.astype(jnp.bfloat16), preferred_element_type=jnp.float32
    )
    keys = jnp.where(hit > 0.5, place, -1.0)
    slot_ids = lax.broadcasted_iota(jnp.int32, (cap, rows), 0).astype(jnp.float32)
    picks = jnp.concatenate(
        [jnp.where(keys[e : e + 1, :] == slot_ids, 1.0, 0.0).astype(jnp.bfloat16) for e in range(n_exp)], axis=0
    )
    for a, source in enumerate((tokens, grads)):
        values = jnp.dot(picks, source[...], preferred_element_type=jnp.float32).astype(jnp.bfloat16)
        packed[a * n_exp : (a + 1) * n_exp] = values.reshape(n_exp, cap, chunk)
        slots[a * n_exp + mine, seq] = packed[a * n_exp + mine]

    own_key = jnp.sum(jnp.where(experts == mine, keys, 0.0), axis=0, keepdims=True)
    own_code = jnp.where(first == mine, codes[0:1, :], 0) + jnp.where(second == mine, codes[1:2, :], 0)
    own_weight = own_code.astype(jnp.float32) / 4096.0
    column = jnp.sum(jnp.where(own_key == slot_ids, own_weight, 0.0), axis=1, keepdims=True)
    diagonal = lax.broadcasted_iota(jnp.int32, (cap, 128), 0) == lax.broadcasted_iota(jnp.int32, (cap, 128), 1)
    row = jnp.sum(jnp.where(diagonal, column, 0.0), axis=0, keepdims=True)
    weight_rows[seq] = jnp.broadcast_to(row, (8, 128))

    pl.semaphore_wait(barrier, n_dp - 1 + n_exp - 1)

    def send_block(src, dst, send_sem, recv_sem, to_seq, to_expert):
        pltpu.make_async_remote_copy(
            src_ref=src, dst_ref=dst, send_sem=send_sem, recv_sem=recv_sem,
            device_id=(to_seq, to_expert), device_id_type=MESH,
        ).start()

    def wait_for(ref, sem):
        pltpu.make_async_copy(ref, ref, sem).wait()

    def peers(k):
        odd = lax.rem(k, 2)
        one, two = [], []
        for step in range(1, side):
            along_x = seq_y * side + lax.rem(seq_x + step, side)
            along_y = lax.rem(seq_y + step, side) * side + seq_x
            one.append(along_x + odd * (along_y - along_x))
            two.append(along_y + odd * (along_x - along_y))
        return one, two

    def send_out(unit):
        a, k, _ = split(unit)

        @pl.when(k > 0)
        def _():
            to = swapped(mine, k, n_exp)
            send_block(
                packed.at[a * n_exp + to], slots.at[a * n_exp + mine, seq],
                send_one, recv_one.at[a * n_exp + mine], seq, to,
            )

    def stage_one(unit):
        a, k, at = split(unit)

        @pl.when(k > 0)
        def _():
            wait_for(slots.at[at, seq], recv_one.at[at])

        one, two = peers(k)
        for to in one:
            send_block(slots.at[at, seq], slots.at[at, seq], send_two, recv_two.at[at], to, mine)
        for to in two:
            send_block(slots.at[at, seq], slots.at[at, seq], send_two, recv_three.at[at], to, mine)

    def stage_two(unit):
        a, k, at = split(unit)
        one, two = peers(k)
        wait_for(slots.at[at, pl.ds(0, side - 1)], recv_two.at[at])
        for source in one:
            for to in two:
                send_block(slots.at[at, source], slots.at[at, source], send_two, recv_three.at[at], to, mine)

    tiles = [slice(n, min(n + TILE, hidden)) for n in range(0, hidden, TILE)]

    def stage_three(unit):
        a, k, at = split(unit)
        j = swapped(mine, k, n_exp)
        wait_for(slots.at[at, pl.ds(0, side * (side - 1))], recv_three.at[at])
        span = pl.ds(pl.multiple_of(j * chunk, chunk), chunk)

        @pl.when(a == 0)
        def _():
            weight_copy(0, j).wait()
            weight_copy(1, j).wait()
            block = slots[at].reshape(total_rows, chunk)
            in_sum[...] += jnp.dot(block, proj_in[span, :], preferred_element_type=jnp.float32)
            turned = block.T
            for part in tiles:
                gate[part] += jnp.dot(gate_w[j, part, :], turned, preferred_element_type=jnp.float32)
                upper[part] += jnp.dot(up_w[j, part, :], turned, preferred_element_type=jnp.float32)

        @pl.when(a == 1)
        def _():
            weight_copy(2, j).wait()
            block = slots[at].reshape(total_rows, chunk)
            out_sum[...] += jnp.dot(block, proj_in[span, :], preferred_element_type=jnp.float32)
            turned = block.T
            for part in tiles:
                back[part] += jnp.dot(down_w[j, part, :], turned, preferred_element_type=jnp.float32)

        @pl.when(unit == units - n_exp // 2 - 1)
        def _():
            for part in tiles:
                g, u = gate[part], upper[part]
                sig = jax.nn.sigmoid(g)
                act = g * sig
                gate[part] = act
                upper[part] = u * sig * (1.0 + g * (1.0 - sig))
                squeezed[part] = (act * u).astype(jnp.bfloat16)
            hid_sum[...] = jnp.dot(proj_hidden[:rank], squeezed[...], preferred_element_type=jnp.float32)

    def loop(low, high, function):
        def body(index, carry):
            function(index)
            return carry

        lax.fori_loop(low, high, body, 0)

    loop(0, AHEAD, send_out)
    for step in range(1, n_dp):
        send_block(weight_rows.at[seq], weight_rows.at[seq], send_row, recv_row, at_seq(step), mine)
    for copy in projections:
        copy.start()
    loop(0, LOADS, load)
    for ref in (gate, upper, back, in_sum, out_sum):
        ref[...] = jnp.zeros_like(ref)
    for copy in projections:
        copy.wait()

    def step_of(step):
        pl.when(step < units)(lambda: stage_one(step))
        pl.when(step < units - AHEAD)(lambda: send_out(step + AHEAD))
        pl.when((step >= RELAY) & (step < units + RELAY))(lambda: stage_two(step - RELAY))
        pl.when(step < units - LOADS)(lambda: load(step + LOADS))
        pl.when(step >= LAG)(lambda: stage_three(step - LAG))

    loop(0, units + LAG, step_of)

    wait_for(weight_rows.at[pl.ds(0, n_dp - 1)], recv_row)
    weight = jnp.concatenate([weight_rows[s, 0:1, :cap] for s in range(n_dp)], axis=1)
    for part in tiles:
        scaled = back[part] * weight
        squeezed[part] = (scaled * gate[part]).astype(jnp.bfloat16)
        other[part] = (scaled * upper[part]).astype(jnp.bfloat16)
    up_proj = jnp.dot(proj_hidden[2 * rank :], squeezed[...], preferred_element_type=jnp.float32)
    gate_proj = jnp.dot(proj_hidden[rank : 2 * rank], other[...], preferred_element_type=jnp.float32)
    in_proj = in_sum[...].T[:rank]
    out_proj = out_sum[...].T[rank:] * weight
    share = 3 * rank // n_dp

    shape = (n_dp * rank, total_rows)
    same = lax.div(lax.broadcasted_iota(jnp.int32, shape, 0), rank) == lax.div(
        lax.broadcasted_iota(jnp.int32, shape, 1), cap
    )

    def product(left, right):
        return lax.dot_general(
            left, right, (((1,), (1,)), ((), ())),
            preferred_element_type=jnp.float32, precision=lax.Precision.HIGHEST,
        )

    left_in = jnp.where(same, jnp.concatenate([in_proj] * n_dp, axis=0), 0.0)
    left_hid = jnp.where(same, jnp.concatenate([hid_sum[...]] * n_dp, axis=0), 0.0)
    products = (product(left_in, gate_proj), product(left_in, up_proj), product(left_hid, out_proj))
    for s in range(n_dp):
        stacked = jnp.concatenate([value[s * rank : (s + 1) * rank] for value in products], axis=0)
        for d in range(n_dp):
            low, mid, high = d * share, d * share + share // 2, (d + 1) * share
            parts[d, s] = jnp.concatenate([stacked[low:mid], stacked[mid:high]], axis=1)
    for step in range(1, n_dp):
        to = at_seq(step)
        send_block(parts.at[to], arrived.at[seq], send_part, recv_part, to, mine)
    arrived[seq] = parts[seq]
    wait_for(arrived.at[pl.ds(0, n_dp - 1)], recv_part)
    result = arrived[0]
    for s in range(1, n_dp):
        result += arrived[s]
    out[...] = jnp.concatenate([result[:, :, :rank], result[:, :, rank:]], axis=1)

    wait_for(packed.at[pl.ds(0, 2 * (n_exp - 1))], send_one)
    wait_for(slots.at[:, pl.ds(0, n_dp - 1)], send_two)
    wait_for(weight_rows.at[pl.ds(0, n_dp - 1)], send_row)
    wait_for(parts.at[pl.ds(0, n_dp - 1)], send_part)


def per_device(tokens, out_grads, routes, gate_codes, w_gate, w_up, w_down, proj_in, proj_hidden):
    n_dp = lax.axis_size("dp")
    n_exp = lax.axis_size("expert")
    rows, chunk = tokens.shape
    cap = rows // 4
    hidden = w_gate.shape[2]
    rank = proj_in.shape[1] // 2
    share = 3 * rank // n_dp
    total = n_dp * cap
    vmem = pl.BlockSpec(memory_space=pltpu.VMEM)
    hbm = pl.BlockSpec(memory_space=pl.ANY)
    f32, bf16 = jnp.float32, jnp.bfloat16
    dma = pltpu.SemaphoreType.DMA
    result = pl.pallas_call(
        functools.partial(kernel, n_dp, n_exp),
        out_shape=jax.ShapeDtypeStruct((n_dp, share, rank), f32),
        in_specs=[vmem, vmem, vmem, vmem, hbm, hbm, hbm, hbm, hbm],
        out_specs=vmem,
        scratch_shapes=[
            pltpu.VMEM((2 * n_exp, cap, chunk), bf16),
            pltpu.VMEM((2 * n_exp, n_dp, cap, chunk), bf16),
            pltpu.VMEM((n_exp, hidden, chunk), bf16),
            pltpu.VMEM((n_exp, hidden, chunk), bf16),
            pltpu.VMEM((n_exp, hidden, chunk), bf16),
            pltpu.VMEM((hidden, total), f32),
            pltpu.VMEM((hidden, total), f32),
            pltpu.VMEM((hidden, total), f32),
            pltpu.VMEM((total, 2 * rank), f32),
            pltpu.VMEM((total, 2 * rank), f32),
            pltpu.VMEM((rank, total), f32),
            pltpu.VMEM((hidden, total), bf16),
            pltpu.VMEM((hidden, total), bf16),
            pltpu.VMEM(proj_in.shape, bf16),
            pltpu.VMEM(proj_hidden.shape[::-1], bf16),
            pltpu.VMEM((n_dp, 8, 128), f32),
            pltpu.VMEM((n_dp, n_dp, share // 2, 2 * rank), f32),
            pltpu.VMEM((n_dp, n_dp, share // 2, 2 * rank), f32),
            dma((3, n_exp)),
            dma((2,)),
            dma, dma((2 * n_exp,)),
            dma, dma((2 * n_exp,)), dma((2 * n_exp,)),
            dma, dma,
            dma, dma,
        ],
        compiler_params=pltpu.CompilerParams(
            collective_id=0, has_side_effects=True, vmem_limit_bytes=60 * 1024 * 1024
        ),
    )(
        tokens, out_grads, routes.T, gate_codes.T, jnp.swapaxes(w_gate, 1, 2), jnp.swapaxes(w_up, 1, 2), w_down,
        proj_in, proj_hidden.T,
    )
    return result.reshape(n_dp, 1, share * rank)


def solution(mesh):
    return jax.shard_map(
        per_device,
        mesh=mesh,
        in_specs=(
            P("dp", "expert"),
            P("dp", "expert"),
            P("dp", None),
            P("dp", None),
            P("expert", None, "dp"),
            P("expert", None, "dp"),
            P("expert", "dp", None),
            P(),
            P("dp", None),
        ),
        out_specs=P(None, "expert", "dp"),
        check_vma=False,
    )
```

```python
import functools
import math

import jax
import jax.numpy as jnp
from jax import lax
from jax.experimental import pallas as pl
from jax.experimental.pallas import tpu as pltpu
from jax.sharding import PartitionSpec as P

MESH = pl.DeviceIdType.MESH
TILE = 400
AHEAD = 8
LOADS = 4
RELAY = 3
LAG = 5


def swapped(a, b, count):
    total, bit = 0, 1
    while bit < count:
        total = total + lax.rem(lax.div(a, bit) + lax.div(b, bit), 2) * bit
        bit *= 2
    return total


def kernel(
    n_dp, n_exp, tokens, grads, routes, codes, w_gate, w_up, w_down, proj_in_hbm, proj_hidden_hbm, out,
    packed, slots, gate_w, up_w, down_w, gate, upper, back, in_sum, out_sum, squeezed, other, turned_in, turned_hid, left_in, left_hid, proj_in, proj_hidden, weight_rows, whole_parts, parts, arrived,
    load_sem, proj_sem, send_one, recv_one, send_two, recv_two, recv_three, send_row, recv_row, send_part, recv_part,
):
    rows, chunk = tokens.shape
    cap = packed.shape[1]
    hidden = gate.shape[0]
    rank = proj_in_hbm.shape[1] // 2
    side = math.isqrt(n_dp)
    units = 2 * n_exp
    total_rows = n_dp * cap
    seq = lax.axis_index("dp")
    mine = lax.axis_index("expert")
    seq_y, seq_x = lax.div(seq, side), lax.rem(seq, side)

    def at_seq(index):
        return lax.rem(seq + index, n_dp)

    barrier = pltpu.get_barrier_semaphore()
    for step in range(1, n_dp):
        pl.semaphore_signal(barrier, inc=1, device_id=(at_seq(step), mine), device_id_type=MESH)
    for step in range(1, n_exp):
        pl.semaphore_signal(
            barrier, inc=1, device_id=(seq, lax.rem(mine + step, n_exp)), device_id_type=MESH
        )

    def weight_copy(which, j):
        span = pl.ds(pl.multiple_of(j * chunk, chunk), chunk)
        source, target = ((w_gate, gate_w), (w_up, up_w), (w_down, down_w))[which]
        return pltpu.make_async_copy(source.at[0, :, span], target.at[j], load_sem.at[which, j])

    projections = (
        pltpu.make_async_copy(proj_in_hbm, proj_in, proj_sem.at[0]),
        pltpu.make_async_copy(proj_hidden_hbm, proj_hidden, proj_sem.at[1]),
    )

    def split(unit):
        base, size, edge = 0, 2, 4
        while edge < units:
            past = lax.div(lax.div(unit, edge) + units, units + 1)
            base = base + past * (edge if edge == 4 else edge // 2)
            size = size + past * (0 if edge == 4 else edge // 4)
            edge *= 2
        within = unit - base
        a = lax.div(within, size)
        k = lax.rem(within, size) + size * lax.div(lax.div(unit, 4) + units, units + 1)
        return a, k, a * n_exp + swapped(mine, k, n_exp)

    def load(unit):
        a, k, _ = split(unit)
        j = swapped(mine, k, n_exp)

        @pl.when(a == 0)
        def _():
            weight_copy(0, j).start()
            weight_copy(1, j).start()

        @pl.when(a == 1)
        def _():
            weight_copy(2, j).start()

    depth = max(16, n_exp)
    experts = lax.broadcasted_iota(jnp.int32, (depth, rows), 0)
    first, second = routes[0:1, :], routes[1:2, :]
    hit = jnp.where((first == experts) | (second == experts), 1.0, 0.0)
    earlier = jnp.where(
        lax.broadcasted_iota(jnp.int32, (rows, rows), 0) < lax.broadcasted_iota(jnp.int32, (rows, rows), 1), 1.0, 0.0
    )
    place = jnp.dot(
        hit.astype(jnp.bfloat16), earlier.astype(jnp.bfloat16), preferred_element_type=jnp.float32
    )
    keys = jnp.where(hit > 0.5, place, -1.0)
    slot_ids = lax.broadcasted_iota(jnp.int32, (cap, rows), 0).astype(jnp.float32)
    picks = jnp.concatenate(
        [jnp.where(keys[e : e + 1, :] == slot_ids, 1.0, 0.0).astype(jnp.bfloat16) for e in range(n_exp)], axis=0
    )
    for a, source in enumerate((tokens, grads)):
        values = jnp.dot(picks, source[...], preferred_element_type=jnp.float32).astype(jnp.bfloat16)
        packed[a * n_exp : (a + 1) * n_exp] = values.reshape(n_exp, cap, chunk)
        slots[a * n_exp + mine, seq] = packed[a * n_exp + mine]

    own_key = jnp.sum(jnp.where(experts == mine, keys, 0.0), axis=0, keepdims=True)
    own_code = jnp.where(first == mine, codes[0:1, :], 0) + jnp.where(second == mine, codes[1:2, :], 0)
    own_weight = own_code.astype(jnp.float32) / 4096.0
    column = jnp.sum(jnp.where(own_key == slot_ids, own_weight, 0.0), axis=1, keepdims=True)
    diagonal = lax.broadcasted_iota(jnp.int32, (cap, 128), 0) == lax.broadcasted_iota(jnp.int32, (cap, 128), 1)
    row = jnp.sum(jnp.where(diagonal, column, 0.0), axis=0, keepdims=True)
    weight_rows[seq] = jnp.broadcast_to(row, (8, 128))

    pl.semaphore_wait(barrier, n_dp - 1 + n_exp - 1)

    def send_block(src, dst, send_sem, recv_sem, to_seq, to_expert):
        pltpu.make_async_remote_copy(
            src_ref=src, dst_ref=dst, send_sem=send_sem, recv_sem=recv_sem,
            device_id=(to_seq, to_expert), device_id_type=MESH,
        ).start()

    def wait_for(ref, sem):
        pltpu.make_async_copy(ref, ref, sem).wait()

    def peers(k):
        odd = lax.rem(k, 2)
        one, two = [], []
        for step in range(1, side):
            along_x = seq_y * side + lax.rem(seq_x + step, side)
            along_y = lax.rem(seq_y + step, side) * side + seq_x
            one.append(along_x + odd * (along_y - along_x))
            two.append(along_y + odd * (along_x - along_y))
        return one, two

    def send_out(unit):
        a, k, _ = split(unit)

        @pl.when(k > 0)
        def _():
            to = swapped(mine, k, n_exp)
            send_block(
                packed.at[a * n_exp + to], slots.at[a * n_exp + mine, seq],
                send_one, recv_one.at[a * n_exp + mine], seq, to,
            )

    def stage_one(unit):
        a, k, at = split(unit)

        @pl.when(k > 0)
        def _():
            wait_for(slots.at[at, seq], recv_one.at[at])

        one, two = peers(k)
        for to in one:
            send_block(slots.at[at, seq], slots.at[at, seq], send_two, recv_two.at[at], to, mine)
        for to in two:
            send_block(slots.at[at, seq], slots.at[at, seq], send_two, recv_three.at[at], to, mine)

    def stage_two(unit):
        a, k, at = split(unit)
        one, two = peers(k)
        wait_for(slots.at[at, pl.ds(0, side - 1)], recv_two.at[at])
        for source in one:
            for to in two:
                send_block(slots.at[at, source], slots.at[at, source], send_two, recv_three.at[at], to, mine)

    tiles = [slice(n, min(n + TILE, hidden)) for n in range(0, hidden, TILE)]

    def halves(value):
        high = value.astype(jnp.bfloat16)
        return high, (value - high.astype(jnp.float32)).astype(jnp.bfloat16)

    def stage_three(unit):
        a, k, at = split(unit)
        j = swapped(mine, k, n_exp)
        wait_for(slots.at[at, pl.ds(0, side * (side - 1))], recv_three.at[at])
        span = pl.ds(pl.multiple_of(j * chunk, chunk), chunk)

        @pl.when(a == 0)
        def _():
            weight_copy(0, j).wait()
            weight_copy(1, j).wait()
            block = slots[at].reshape(total_rows, chunk)
            in_sum[...] += jnp.dot(block, proj_in[span, :], preferred_element_type=jnp.float32)
            turned = block.T
            for part in tiles:
                gate[part] += jnp.dot(gate_w[j, part, :], turned, preferred_element_type=jnp.float32)
                upper[part] += jnp.dot(up_w[j, part, :], turned, preferred_element_type=jnp.float32)

        @pl.when(a == 1)
        def _():
            weight_copy(2, j).wait()
            block = slots[at].reshape(total_rows, chunk)
            out_sum[...] += jnp.dot(block, proj_in[span, :], preferred_element_type=jnp.float32)
            turned = block.T
            for part in tiles:
                back[part] += jnp.dot(down_w[j, part, :], turned, preferred_element_type=jnp.float32)

        @pl.when(unit == units - n_exp // 2 - 1)
        def _():
            for part in tiles:
                g, u = gate[part], upper[part]
                sig = jax.nn.sigmoid(g)
                act = g * sig
                gate[part] = act
                upper[part] = u * sig * (1.0 + g * (1.0 - sig))
                squeezed[part] = (act * u).astype(jnp.bfloat16)
            hid_proj = jnp.dot(proj_hidden[:rank], squeezed[...], preferred_element_type=jnp.float32)
            in_proj = in_sum[...].T[:rank]
            for piece in range(turned_in.shape[0]):
                lanes = slice(piece * turned_in.shape[2], (piece + 1) * turned_in.shape[2])
                turned_in[piece] = in_proj[:, lanes]
                turned_hid[piece] = hid_proj[:, lanes]
            half = rank // 2
            shape = (n_dp * rank, total_rows)
            row_seq = lax.div(lax.rem(lax.broadcasted_iota(jnp.int32, shape, 0), n_dp * half), half)
            same = row_seq == lax.div(lax.broadcasted_iota(jnp.int32, shape, 1), cap)
            for target, source in ((left_in, turned_in), (left_hid, turned_hid)):
                even, odd = (
                    jnp.concatenate(
                        [source[piece, pl.ds(parity, half, stride=2), :] for piece in range(source.shape[0])], axis=1
                    )
                    for parity in range(2)
                )
                spread = jnp.concatenate([even] * n_dp + [odd] * n_dp, axis=0)
                high, low = halves(jnp.where(same, spread, 0.0))
                target[...] = jnp.concatenate([high, low, high], axis=1)

    def loop(low, high, function):
        def body(index, carry):
            function(index)
            return carry

        lax.fori_loop(low, high, body, 0)

    loop(0, AHEAD, send_out)
    for step in range(1, n_dp):
        send_block(weight_rows.at[seq], weight_rows.at[seq], send_row, recv_row, at_seq(step), mine)
    for copy in projections:
        copy.start()
    loop(0, LOADS, load)
    for ref in (gate, upper, back, in_sum, out_sum):
        ref[...] = jnp.zeros_like(ref)
    for copy in projections:
        copy.wait()

    def step_of(step):
        pl.when(step < units)(lambda: stage_one(step))
        pl.when(step < units - AHEAD)(lambda: send_out(step + AHEAD))
        pl.when((step >= RELAY) & (step < units + RELAY))(lambda: stage_two(step - RELAY))
        pl.when(step < units - LOADS)(lambda: load(step + LOADS))
        pl.when(step >= LAG)(lambda: stage_three(step - LAG))

    loop(0, units + LAG, step_of)

    wait_for(weight_rows.at[pl.ds(0, n_dp - 1)], recv_row)
    weight = jnp.concatenate([weight_rows[s, 0:1, :cap] for s in range(n_dp)], axis=1)
    for part in tiles:
        scaled = back[part] * weight
        squeezed[part] = (scaled * gate[part]).astype(jnp.bfloat16)
        other[part] = (scaled * upper[part]).astype(jnp.bfloat16)
    up_proj = jnp.dot(proj_hidden[2 * rank :], squeezed[...], preferred_element_type=jnp.float32)
    gate_proj = jnp.dot(proj_hidden[rank : 2 * rank], other[...], preferred_element_type=jnp.float32)
    out_proj = out_sum[...].T[rank:] * weight
    half = rank // 2
    share = 3 * half // n_dp

    def product(left, right):
        high, low = halves(right)
        value = lax.dot_general(
            left[...], jnp.concatenate([high, high, low], axis=1), (((1,), (1,)), ((), ())),
            preferred_element_type=jnp.float32,
        )
        return jnp.concatenate([value[: n_dp * half], value[n_dp * half :]], axis=1)

    products = (product(left_in, gate_proj), product(left_in, up_proj), product(left_hid, out_proj))
    stacked = [
        jnp.concatenate([value[s * half : (s + 1) * half] for value in products], axis=0) for s in range(n_dp)
    ]
    for d in range(n_dp):
        block = jnp.concatenate([value[d * share : (d + 1) * share] for value in stacked], axis=0)
        whole_parts[d] = block
        parts[d] = block.astype(jnp.bfloat16)
    for step in range(1, n_dp):
        to = at_seq(step)
        send_block(parts.at[to], arrived.at[seq], send_part, recv_part, to, mine)
    wait_for(arrived.at[pl.ds(0, n_dp - 1)], recv_part)
    result = whole_parts[seq]
    for step in range(1, n_dp):
        result += arrived[at_seq(step)].astype(jnp.float32)
    out[...] = result

    wait_for(packed.at[pl.ds(0, 2 * (n_exp - 1))], send_one)
    wait_for(slots.at[:, pl.ds(0, n_dp - 1)], send_two)
    wait_for(weight_rows.at[pl.ds(0, n_dp - 1)], send_row)
    wait_for(parts.at[pl.ds(0, n_dp - 1)], send_part)


def per_device(tokens, out_grads, routes, gate_codes, w_gate, w_up, w_down, proj_in, proj_hidden):
    n_dp = lax.axis_size("dp")
    n_exp = lax.axis_size("expert")
    rows, chunk = tokens.shape
    cap = rows // 4
    hidden = w_gate.shape[2]
    rank = proj_in.shape[1] // 2
    share = 3 * rank // n_dp
    total = n_dp * cap
    lanes = min(128, total)
    vmem = pl.BlockSpec(memory_space=pltpu.VMEM)
    hbm = pl.BlockSpec(memory_space=pl.ANY)
    f32, bf16 = jnp.float32, jnp.bfloat16
    dma = pltpu.SemaphoreType.DMA
    result = pl.pallas_call(
        functools.partial(kernel, n_dp, n_exp),
        out_shape=jax.ShapeDtypeStruct((3 * rank // 2, 2 * rank), f32),
        in_specs=[vmem, vmem, vmem, vmem, hbm, hbm, hbm, hbm, hbm],
        out_specs=vmem,
        scratch_shapes=[
            pltpu.VMEM((2 * n_exp, cap, chunk), bf16),
            pltpu.VMEM((2 * n_exp, n_dp, cap, chunk), bf16),
            pltpu.VMEM((n_exp, hidden, chunk), bf16),
            pltpu.VMEM((n_exp, hidden, chunk), bf16),
            pltpu.VMEM((n_exp, hidden, chunk), bf16),
            pltpu.VMEM((hidden, total), f32),
            pltpu.VMEM((hidden, total), f32),
            pltpu.VMEM((hidden, total), f32),
            pltpu.VMEM((total, 2 * rank), f32),
            pltpu.VMEM((total, 2 * rank), f32),
            pltpu.VMEM((hidden, total), bf16),
            pltpu.VMEM((hidden, total), bf16),
            pltpu.VMEM((total // lanes, rank, lanes), f32),
            pltpu.VMEM((total // lanes, rank, lanes), f32),
            pltpu.VMEM((n_dp * rank, 3 * total), bf16),
            pltpu.VMEM((n_dp * rank, 3 * total), bf16),
            pltpu.VMEM(proj_in.shape, bf16),
            pltpu.VMEM(proj_hidden.shape[::-1], bf16),
            pltpu.VMEM((n_dp, 8, 128), f32),
            pltpu.VMEM((n_dp, 3 * rank // 2, 2 * rank), f32),
            pltpu.VMEM((n_dp, 3 * rank // 2, 2 * rank), bf16),
            pltpu.VMEM((n_dp, 3 * rank // 2, 2 * rank), bf16),
            dma((3, n_exp)),
            dma((2,)),
            dma, dma((2 * n_exp,)),
            dma, dma((2 * n_exp,)), dma((2 * n_exp,)),
            dma, dma,
            dma, dma,
        ],
        compiler_params=pltpu.CompilerParams(
            collective_id=0, has_side_effects=True, vmem_limit_bytes=60 * 1024 * 1024
        ),
    )(
        tokens, out_grads, routes.T, gate_codes.T, jnp.swapaxes(w_gate, 1, 2), jnp.swapaxes(w_up, 1, 2), w_down,
        proj_in, proj_hidden.T,
    )
    return result.reshape(n_dp, 1, share * rank)


def solution(mesh):
    return jax.shard_map(
        per_device,
        mesh=mesh,
        in_specs=(
            P("dp", "expert"),
            P("dp", "expert"),
            P("dp", None),
            P("dp", None),
            P("expert", None, "dp"),
            P("expert", None, "dp"),
            P("expert", "dp", None),
            P(),
            P("dp", None),
        ),
        out_specs=P(None, "expert", "dp"),
        check_vma=False,
    )
```

```python
import functools
import math

import jax
import jax.numpy as jnp
from jax import lax
from jax.experimental import pallas as pl
from jax.experimental.pallas import tpu as pltpu
from jax.sharding import PartitionSpec as P

MESH = pl.DeviceIdType.MESH
TILE = 400
AHEAD = 12
LOADS = 4
RELAY = 3
LAG = 5


def swapped(a, b, count):
    total, bit = 0, 1
    while bit < count:
        total = total + lax.rem(lax.div(a, bit) + lax.div(b, bit), 2) * bit
        bit *= 2
    return total


def kernel(
    n_dp, n_exp, tokens, grads, routes, codes, w_gate, w_up, w_down, proj_in_hbm, proj_hidden_hbm, out,
    packed, slots, gate_w, up_w, down_w, gate, upper, back, in_sum, out_sum, squeezed, other, turned_in, turned_hid, left_in, left_hid, proj_in, proj_hidden, weight_rows, whole_parts, parts, arrived,
    load_sem, proj_sem, send_one, recv_one, send_two, recv_two, recv_three, send_row, recv_row, send_part, recv_part,
):
    rows, chunk = tokens.shape
    cap = packed.shape[1]
    hidden = gate.shape[0]
    rank = proj_in_hbm.shape[1] // 2
    side = math.isqrt(n_dp)
    units = 2 * n_exp
    total_rows = n_dp * cap
    seq = lax.axis_index("dp")
    mine = lax.axis_index("expert")
    seq_y, seq_x = lax.div(seq, side), lax.rem(seq, side)

    def at_seq(index):
        return lax.rem(seq + index, n_dp)

    barrier = pltpu.get_barrier_semaphore()
    for step in range(1, n_dp):
        pl.semaphore_signal(barrier, inc=1, device_id=(at_seq(step), mine), device_id_type=MESH)
    for step in range(1, n_exp):
        pl.semaphore_signal(
            barrier, inc=1, device_id=(seq, lax.rem(mine + step, n_exp)), device_id_type=MESH
        )

    def weight_copy(which, j):
        span = pl.ds(pl.multiple_of(j * chunk, chunk), chunk)
        source, target = ((w_gate, gate_w), (w_up, up_w), (w_down, down_w))[which]
        return pltpu.make_async_copy(source.at[0, :, span], target.at[j], load_sem.at[which, j])

    projections = (
        pltpu.make_async_copy(proj_in_hbm, proj_in, proj_sem.at[0]),
        pltpu.make_async_copy(proj_hidden_hbm, proj_hidden, proj_sem.at[1]),
    )

    def split(unit):
        base, size, edge = 0, 2, 4
        while edge < units:
            past = lax.div(lax.div(unit, edge) + units, units + 1)
            base = base + past * (edge if edge == 4 else edge // 2)
            size = size + past * (0 if edge == 4 else edge // 4)
            edge *= 2
        within = unit - base
        a = lax.div(within, size)
        k = lax.rem(within, size) + size * lax.div(lax.div(unit, 4) + units, units + 1)
        return a, k, a * n_exp + swapped(mine, k, n_exp)

    def load(unit):
        a, k, _ = split(unit)
        j = swapped(mine, k, n_exp)

        @pl.when(a == 0)
        def _():
            weight_copy(0, j).start()
            weight_copy(1, j).start()

        @pl.when(a == 1)
        def _():
            weight_copy(2, j).start()

    depth = max(16, n_exp)
    experts = lax.broadcasted_iota(jnp.int32, (depth, rows), 0)
    first, second = routes[0:1, :], routes[1:2, :]
    hit = jnp.where((first == experts) | (second == experts), 1.0, 0.0)
    earlier = jnp.where(
        lax.broadcasted_iota(jnp.int32, (rows, rows), 0) < lax.broadcasted_iota(jnp.int32, (rows, rows), 1), 1.0, 0.0
    )
    place = jnp.dot(
        hit.astype(jnp.bfloat16), earlier.astype(jnp.bfloat16), preferred_element_type=jnp.float32
    )
    keys = jnp.where(hit > 0.5, place, -1.0)
    slot_ids = lax.broadcasted_iota(jnp.int32, (cap, rows), 0).astype(jnp.float32)
    picks = jnp.concatenate(
        [jnp.where(keys[e : e + 1, :] == slot_ids, 1.0, 0.0).astype(jnp.bfloat16) for e in range(n_exp)], axis=0
    )
    for a, source in enumerate((tokens, grads)):
        values = jnp.dot(picks, source[...], preferred_element_type=jnp.float32).astype(jnp.bfloat16)
        packed[a * n_exp : (a + 1) * n_exp] = values.reshape(n_exp, cap, chunk)
        slots[a * n_exp + mine, seq] = packed[a * n_exp + mine]

    own_key = jnp.sum(jnp.where(experts == mine, keys, 0.0), axis=0, keepdims=True)
    own_code = jnp.where(first == mine, codes[0:1, :], 0) + jnp.where(second == mine, codes[1:2, :], 0)
    own_weight = own_code.astype(jnp.float32) / 4096.0
    column = jnp.sum(jnp.where(own_key == slot_ids, own_weight, 0.0), axis=1, keepdims=True)
    diagonal = lax.broadcasted_iota(jnp.int32, (cap, 128), 0) == lax.broadcasted_iota(jnp.int32, (cap, 128), 1)
    row = jnp.sum(jnp.where(diagonal, column, 0.0), axis=0, keepdims=True)
    weight_rows[seq] = jnp.broadcast_to(row, (8, 128))

    pl.semaphore_wait(barrier, n_dp - 1 + n_exp - 1)

    def send_block(src, dst, send_sem, recv_sem, to_seq, to_expert):
        pltpu.make_async_remote_copy(
            src_ref=src, dst_ref=dst, send_sem=send_sem, recv_sem=recv_sem,
            device_id=(to_seq, to_expert), device_id_type=MESH,
        ).start()

    def wait_for(ref, sem):
        pltpu.make_async_copy(ref, ref, sem).wait()

    def peers(k):
        odd = lax.rem(k + mine, 2)
        one, two = [], []
        for step in range(1, side):
            along_x = seq_y * side + lax.rem(seq_x + step, side)
            along_y = lax.rem(seq_y + step, side) * side + seq_x
            one.append(along_x + odd * (along_y - along_x))
            two.append(along_y + odd * (along_x - along_y))
        return one, two

    def send_out(unit):
        a, k, _ = split(unit)

        @pl.when(k > 0)
        def _():
            to = swapped(mine, k, n_exp)
            send_block(
                packed.at[a * n_exp + to], slots.at[a * n_exp + mine, seq],
                send_one, recv_one.at[a * n_exp + mine], seq, to,
            )

    def stage_one(unit):
        a, k, at = split(unit)

        @pl.when(k > 0)
        def _():
            wait_for(slots.at[at, seq], recv_one.at[at])

        one, two = peers(k)
        for to in one:
            send_block(slots.at[at, seq], slots.at[at, seq], send_two, recv_two.at[at], to, mine)
        for to in two:
            send_block(slots.at[at, seq], slots.at[at, seq], send_two, recv_three.at[at], to, mine)

    def stage_two(unit):
        a, k, at = split(unit)
        one, two = peers(k)
        wait_for(slots.at[at, pl.ds(0, side - 1)], recv_two.at[at])
        for source in one:
            for to in two:
                send_block(slots.at[at, source], slots.at[at, source], send_two, recv_three.at[at], to, mine)

    tiles = [slice(n, min(n + TILE, hidden)) for n in range(0, hidden, TILE)]

    def halves(value):
        high = value.astype(jnp.bfloat16)
        return high, (value - high.astype(jnp.float32)).astype(jnp.bfloat16)

    def stage_three(unit):
        a, k, at = split(unit)
        j = swapped(mine, k, n_exp)
        wait_for(slots.at[at, pl.ds(0, side * (side - 1))], recv_three.at[at])
        span = pl.ds(pl.multiple_of(j * chunk, chunk), chunk)

        @pl.when(a == 0)
        def _():
            weight_copy(0, j).wait()
            weight_copy(1, j).wait()
            block = slots[at].reshape(total_rows, chunk)
            in_sum[...] += jnp.dot(block, proj_in[span, :], preferred_element_type=jnp.float32)
            turned = block.T
            for part in tiles:
                gate[part] += jnp.dot(gate_w[j, part, :], turned, preferred_element_type=jnp.float32)
                upper[part] += jnp.dot(up_w[j, part, :], turned, preferred_element_type=jnp.float32)

        @pl.when(a == 1)
        def _():
            weight_copy(2, j).wait()
            block = slots[at].reshape(total_rows, chunk)
            out_sum[...] += jnp.dot(block, proj_in[span, :], preferred_element_type=jnp.float32)
            turned = block.T
            for part in tiles:
                back[part] += jnp.dot(down_w[j, part, :], turned, preferred_element_type=jnp.float32)

        @pl.when(unit == units - n_exp // 2 - 1)
        def _():
            for part in tiles:
                g, u = gate[part], upper[part]
                sig = jax.nn.sigmoid(g)
                act = g * sig
                gate[part] = act
                upper[part] = u * sig * (1.0 + g * (1.0 - sig))
                squeezed[part] = (act * u).astype(jnp.bfloat16)
            hid_proj = jnp.dot(proj_hidden[:rank], squeezed[...], preferred_element_type=jnp.float32)
            in_proj = in_sum[...].T[:rank]
            for piece in range(turned_in.shape[0]):
                lanes = slice(piece * turned_in.shape[2], (piece + 1) * turned_in.shape[2])
                turned_in[piece] = in_proj[:, lanes]
                turned_hid[piece] = hid_proj[:, lanes]
            half = rank // 2
            shape = (n_dp * rank, total_rows)
            row_seq = lax.div(lax.rem(lax.broadcasted_iota(jnp.int32, shape, 0), n_dp * half), half)
            same = row_seq == lax.div(lax.broadcasted_iota(jnp.int32, shape, 1), cap)
            for target, source in ((left_in, turned_in), (left_hid, turned_hid)):
                even, odd = (
                    jnp.concatenate(
                        [source[piece, pl.ds(parity, half, stride=2), :] for piece in range(source.shape[0])], axis=1
                    )
                    for parity in range(2)
                )
                spread = jnp.concatenate([even] * n_dp + [odd] * n_dp, axis=0)
                high, low = halves(jnp.where(same, spread, 0.0))
                target[...] = jnp.concatenate([high, low, high], axis=1)

    def loop(low, high, function):
        def body(index, carry):
            function(index)
            return carry

        lax.fori_loop(low, high, body, 0)

    stage_one(0)
    loop(1, 4, send_out)
    for unit in range(4, 8):
        send_out(unit)
        send_out(unit + 4)
    for step in range(1, n_dp):
        send_block(weight_rows.at[seq], weight_rows.at[seq], send_row, recv_row, at_seq(step), mine)
    for copy in projections:
        copy.start()
    loop(0, LOADS, load)
    for ref in (gate, upper, back, in_sum, out_sum):
        ref[...] = jnp.zeros_like(ref)
    for copy in projections:
        copy.wait()

    def step_of(step):
        pl.when((step >= 1) & (step < units))(lambda: stage_one(step))
        pl.when(step < units - AHEAD)(lambda: send_out(step + AHEAD))
        pl.when((step >= RELAY) & (step < units + RELAY))(lambda: stage_two(step - RELAY))
        pl.when(step < units - LOADS)(lambda: load(step + LOADS))
        pl.when(step >= LAG)(lambda: stage_three(step - LAG))

    loop(0, units + LAG, step_of)

    wait_for(weight_rows.at[pl.ds(0, n_dp - 1)], recv_row)
    weight = jnp.concatenate([weight_rows[s, 0:1, :cap] for s in range(n_dp)], axis=1)
    for part in tiles:
        scaled = back[part] * weight
        squeezed[part] = (scaled * gate[part]).astype(jnp.bfloat16)
        other[part] = (scaled * upper[part]).astype(jnp.bfloat16)
    up_proj = jnp.dot(proj_hidden[2 * rank :], squeezed[...], preferred_element_type=jnp.float32)
    gate_proj = jnp.dot(proj_hidden[rank : 2 * rank], other[...], preferred_element_type=jnp.float32)
    out_proj = out_sum[...].T[rank:] * weight
    half = rank // 2
    share = 3 * half // n_dp

    def product(left, right):
        high, low = halves(right)
        value = lax.dot_general(
            left[...], jnp.concatenate([high, high, low], axis=1), (((1,), (1,)), ((), ())),
            preferred_element_type=jnp.float32,
        )
        return jnp.concatenate([value[: n_dp * half], value[n_dp * half :]], axis=1)

    products = (product(left_in, gate_proj), product(left_in, up_proj), product(left_hid, out_proj))
    stacked = [
        jnp.concatenate([value[s * half : (s + 1) * half] for value in products], axis=0) for s in range(n_dp)
    ]
    for d in range(n_dp):
        block = jnp.concatenate([value[d * share : (d + 1) * share] for value in stacked], axis=0)
        whole_parts[d] = block
        parts[d] = block.astype(jnp.bfloat16)
    for step in range(1, n_dp):
        to = at_seq(step)
        send_block(parts.at[to], arrived.at[seq], send_part, recv_part, to, mine)
    wait_for(arrived.at[pl.ds(0, n_dp - 1)], recv_part)
    result = whole_parts[seq]
    for step in range(1, n_dp):
        result += arrived[at_seq(step)].astype(jnp.float32)
    out[...] = result

    wait_for(packed.at[pl.ds(0, 2 * (n_exp - 1))], send_one)
    wait_for(slots.at[:, pl.ds(0, n_dp - 1)], send_two)
    wait_for(weight_rows.at[pl.ds(0, n_dp - 1)], send_row)
    wait_for(parts.at[pl.ds(0, n_dp - 1)], send_part)


def per_device(tokens, out_grads, routes, gate_codes, w_gate, w_up, w_down, proj_in, proj_hidden):
    n_dp = lax.axis_size("dp")
    n_exp = lax.axis_size("expert")
    rows, chunk = tokens.shape
    cap = rows // 4
    hidden = w_gate.shape[2]
    rank = proj_in.shape[1] // 2
    share = 3 * rank // n_dp
    total = n_dp * cap
    lanes = min(128, total)
    vmem = pl.BlockSpec(memory_space=pltpu.VMEM)
    hbm = pl.BlockSpec(memory_space=pl.ANY)
    f32, bf16 = jnp.float32, jnp.bfloat16
    dma = pltpu.SemaphoreType.DMA
    result = pl.pallas_call(
        functools.partial(kernel, n_dp, n_exp),
        out_shape=jax.ShapeDtypeStruct((3 * rank // 2, 2 * rank), f32),
        in_specs=[vmem, vmem, vmem, vmem, hbm, hbm, hbm, hbm, hbm],
        out_specs=vmem,
        scratch_shapes=[
            pltpu.VMEM((2 * n_exp, cap, chunk), bf16),
            pltpu.VMEM((2 * n_exp, n_dp, cap, chunk), bf16),
            pltpu.VMEM((n_exp, hidden, chunk), bf16),
            pltpu.VMEM((n_exp, hidden, chunk), bf16),
            pltpu.VMEM((n_exp, hidden, chunk), bf16),
            pltpu.VMEM((hidden, total), f32),
            pltpu.VMEM((hidden, total), f32),
            pltpu.VMEM((hidden, total), f32),
            pltpu.VMEM((total, 2 * rank), f32),
            pltpu.VMEM((total, 2 * rank), f32),
            pltpu.VMEM((hidden, total), bf16),
            pltpu.VMEM((hidden, total), bf16),
            pltpu.VMEM((total // lanes, rank, lanes), f32),
            pltpu.VMEM((total // lanes, rank, lanes), f32),
            pltpu.VMEM((n_dp * rank, 3 * total), bf16),
            pltpu.VMEM((n_dp * rank, 3 * total), bf16),
            pltpu.VMEM(proj_in.shape, bf16),
            pltpu.VMEM(proj_hidden.shape[::-1], bf16),
            pltpu.VMEM((n_dp, 8, 128), f32),
            pltpu.VMEM((n_dp, 3 * rank // 2, 2 * rank), f32),
            pltpu.VMEM((n_dp, 3 * rank // 2, 2 * rank), bf16),
            pltpu.VMEM((n_dp, 3 * rank // 2, 2 * rank), bf16),
            dma((3, n_exp)),
            dma((2,)),
            dma, dma((2 * n_exp,)),
            dma, dma((2 * n_exp,)), dma((2 * n_exp,)),
            dma, dma,
            dma, dma,
        ],
        compiler_params=pltpu.CompilerParams(
            collective_id=0, has_side_effects=True, vmem_limit_bytes=60 * 1024 * 1024
        ),
    )(
        tokens, out_grads, routes.T, gate_codes.T, jnp.swapaxes(w_gate, 1, 2), jnp.swapaxes(w_up, 1, 2), w_down,
        proj_in, proj_hidden.T,
    )
    return result.reshape(n_dp, 1, share * rank)


def solution(mesh):
    return jax.shard_map(
        per_device,
        mesh=mesh,
        in_specs=(
            P("dp", "expert"),
            P("dp", "expert"),
            P("dp", None),
            P("dp", None),
            P("expert", None, "dp"),
            P("expert", None, "dp"),
            P("expert", "dp", None),
            P(),
            P("dp", None),
        ),
        out_specs=P(None, "expert", "dp"),
        check_vma=False,
    )
```
